1024 devices in a mesh: expert: 64 (over z, x), dp: 16 (over y, core).
Axes of the slice: x: 8, y: 8, z: 8, core: 2. Of those that a mesh axis runs over, the one named last changes fastest.
Arguments:
- tokens: bfloat16 [8192, 7168], P('expert', 'dp'), may hold values from -6 to 6
- routes: int32 [8192, 1], P('expert'), may hold values from 0 to 15; in each aligned block of 128 rows (0 to 127, 128 to 255, ...) at most 10 rows name the same one
- route_weight: bfloat16 [8192, 1], P('expert'), may hold values from 0.099609375 to 1
- out_grad: bfloat16 [8192, 7168], P('expert', 'dp'), may hold values from -0.29882812 to 0.29882812
- w_gate: bfloat16 [7168, 32768], P('dp', 'expert'), may hold values from -0.0625 to 0.0625
- w_up: bfloat16 [7168, 32768], P('dp', 'expert'), may hold values from -0.0625 to 0.0625
- w_down: bfloat16 [32768, 7168], P('expert', 'dp'), may hold values from -0.125 to 0.125
Outputs:
- grad_gate: bfloat16 [7168, 32768], P('dp', 'expert')
- grad_up: bfloat16 [7168, 32768], P('dp', 'expert')
The draws below stay inside these ranges and needn't reach their ends.
Inputs may be any that keep to these rules, and one draw needn't show every extreme that they name: In each aligned block of 128 tokens, the tokens of one index of expert, no expert is named by more than 10 routes, and in every draw some block has an expert named by exactly 10. A token's routes name different experts.
All inputs are finite; a program needn't handle non-finite values.
Results may differ from the reference program's by a relative error of at most 0.035.
Values may be sent and summed in bfloat16 or wider, within the bound.
No kernel may reach another device: no remote copies, remote signals or barrier semaphores. Data moves between devices by JAX's collectives and lax.ppermute only.
A program may use at most 32 MiB of HBM per device.

```python
import math
import jax
import jax.numpy as jnp
import numpy as np
from jax import lax

D = 7168
F = 2048
ROUTES = 1
TOK_DEV = 128
EXPERTS = 16
CAP = 10
TOKENS = 8192
N_EXPERT = 64
N_DP = 16


def levels(rng, dims, split, smallest, largest):
    gain = 1.0
    for dim, shards_of in split:
        heights = jax.random.uniform(jax.random.fold_in(jax.random.fold_in(rng, 6), dim), (shards_of,), jnp.float32, smallest / len(split), largest / len(split))
        gain = gain * jnp.repeat(jnp.exp(heights), dims[dim] // shards_of).reshape((-1,) + (1,) * (len(dims) - 1 - dim))
    return gain


def routed_block(stream_key, own, number, rows, amount, top, bound, lean):
    ranking = jax.random.permutation(stream_key, amount)
    packed, ordinary = load_shares(amount, rows * top, bound, lean, True), load_shares(amount, rows * top, bound, lean, False)
    places = jnp.arange(amount)

    def named(lengths, offset_by):
        used = int((lengths > 0).sum())
        fixed = max(1, used // 4)
        moved = fixed + (places - fixed + offset_by * (used - fixed)) % max(1, amount - fixed)
        return jnp.zeros((amount,), jnp.int32).at[ranking[jnp.where(places < fixed, places, moved)]].set(jnp.asarray(lengths, jnp.int32))

    lengths = jnp.where(number % 4 == 0, named(packed, number // 4), named(ordinary, number - number // 4 - 1))
    mixed = jax.random.permutation(jax.random.fold_in(own, 3), amount)
    donor, sink = mixed[0:amount // 2 * 2:2], mixed[1:amount // 2 * 2:2]
    slack = jnp.minimum(lengths[donor] - 1, bound - lengths[sink]) // 2
    slack = jnp.where((donor == ranking[0]) | (sink == ranking[0]) | (lengths[sink] == 0), 0, jnp.maximum(slack, 0))
    moved = jax.random.randint(jax.random.fold_in(own, 4), (amount // 2,), 0, 1 << 20) % (slack + 1)
    lengths = lengths.at[donor].add(-moved).at[sink].add(moved)
    labels = jnp.searchsorted(jnp.cumsum(lengths), jnp.arange(rows * top), side="right").astype(jnp.int32)
    grid = labels.reshape(top, rows).T
    grid = grid[jax.random.permutation(jax.random.fold_in(own, 1), rows)]
    offset_by = jax.random.randint(jax.random.fold_in(own, 2), (rows, 1), 0, top)
    return jnp.take_along_axis(grid, (jnp.arange(top)[None, :] + offset_by) % top, axis=1)


def load_shares(amount, total, most, slope, full):
    portions = [(1 << 20) // math.isqrt(grade ** slope) + 1 for grade in range(1, amount + 1)]
    largest = most if full else min(most, max(-(-total // amount), total * portions[0] // sum(portions)))
    least = 1 if total - largest >= amount - 1 else 0
    counts, surplus = [largest] + [least] * (amount - 1), total - largest - least * (amount - 1)
    while surplus > 0:
        free = [i for i in range(1, amount) if counts[i] < largest] or [i for i in range(1, amount) if counts[i] < most]
        whole, budget = sum([portions[i] for i in free]), surplus
        for i in free:
            extra = min(most - counts[i], max(1, budget * portions[i] // whole), surplus)
            counts[i] = counts[i] + extra
            surplus = surplus - extra
    return np.array(counts)


def gaussian(stream_key, dims, spread, limit, split=(), held_as=jnp.bfloat16):
    factor_of = levels(stream_key, dims, split, -0.22, 0.18) if split else 1.0
    values = jax.random.normal(stream_key, dims, jnp.float32) * spread * factor_of
    return jnp.minimum(jnp.maximum(values, -limit), limit).astype(held_as)


def setup_inputs(seed: int = 0) -> dict:
    arg_keys = jax.random.split(jax.random.key(seed), 8)
    tokens = gaussian(arg_keys[0], (TOKENS, D), 1.0, 6.0, ((0, 64), (1, 16)))
    routes_keys = jax.random.split(jax.random.fold_in(arg_keys[1], 1), TOKENS // TOK_DEV)
    routes_turns = jax.random.permutation(jax.random.fold_in(arg_keys[1], 3), TOKENS // TOK_DEV)
    routes = jax.vmap(lambda own, number: routed_block(jax.random.fold_in(arg_keys[1], 2), own, number, TOK_DEV, EXPERTS, ROUTES, CAP, 2))(routes_keys, routes_turns).reshape((TOKENS, ROUTES))
    route_weight = jnp.clip(0.099609375 + 0.9003906 * jax.random.uniform(arg_keys[2], (TOKENS, ROUTES), jnp.float32) ** levels(arg_keys[2], (TOKENS, ROUTES), ((0, 64),), -0.2, 0.2), 0.099609375, 1.0).astype(jnp.bfloat16)
    out_grad = gaussian(arg_keys[3], (TOKENS, D), 0.05, 0.29882812, ((0, 64), (1, 16)))
    w_gate = gaussian(arg_keys[4], (D, EXPERTS * F), D ** -0.5, 0.0625, ((0, 16), (1, 64)))
    w_up = gaussian(arg_keys[5], (D, EXPERTS * F), D ** -0.5, 0.0625, ((0, 16), (1, 64)))
    w_down = gaussian(arg_keys[6], (EXPERTS * F, D), F ** -0.5, 0.125, ((0, 64), (1, 16)))
    return {"tokens": tokens, "routes": routes, "route_weight": route_weight, "out_grad": out_grad, "w_gate": w_gate, "w_up": w_up, "w_down": w_down}


def reference(tokens, routes, route_weight, out_grad, w_gate, w_up, w_down):
    width_part = D // N_DP
    slots = N_EXPERT * CAP
    per_group = TOK_DEV * ROUTES
    entries = routes.reshape(N_EXPERT, per_group).astype(jnp.int32)
    onehot = (entries[:, :, None] == jnp.arange(EXPERTS, dtype=jnp.int32)[None, None, :]).astype(jnp.int32)
    before = jnp.cumsum(onehot, axis=1) - onehot
    slot_of = jnp.sum(onehot * before, axis=2).astype(jnp.int32)
    groups = jnp.arange(N_EXPERT, dtype=jnp.int32)[:, None]
    position = (groups * CAP + slot_of).astype(jnp.int32)
    token_ids = (groups * TOK_DEV + (jnp.arange(per_group, dtype=jnp.int32) // ROUTES)[None, :]).astype(jnp.int32)
    token_of = jnp.zeros((EXPERTS, slots), jnp.int32).at[entries, position].set(token_ids)
    live = jnp.zeros((EXPERTS, slots), jnp.float32).at[entries, position].set(jnp.float32(1.0))
    coef = jnp.zeros((EXPERTS, slots), jnp.float32).at[entries, position].set(route_weight.reshape(N_EXPERT, per_group).astype(jnp.float32))

    def one_expert(expert_id):
        index = token_of[expert_id]
        gate_cols = lax.dynamic_slice_in_dim(w_gate, expert_id * F, F, 1)
        up_cols = lax.dynamic_slice_in_dim(w_up, expert_id * F, F, 1)
        down_rows = lax.dynamic_slice_in_dim(w_down, expert_id * F, F, 0)
        token_rows = (tokens[index].astype(jnp.float32) * live[expert_id][:, None]).astype(jnp.bfloat16)
        cotan_rows = (coef[expert_id][:, None] * out_grad[index].astype(jnp.float32)).astype(jnp.bfloat16)
        token_blocks = token_rows.reshape(slots, N_DP, width_part).transpose(1, 0, 2)
        cotan_blocks = cotan_rows.reshape(slots, N_DP, width_part).transpose(1, 0, 2)
        gate_blocks = gate_cols.reshape(N_DP, width_part, F)
        up_blocks = up_cols.reshape(N_DP, width_part, F)
        down_blocks = down_rows.reshape(F, N_DP, width_part).transpose(1, 0, 2)

        def add_block(running, piece):
            token_part, cotan_part, gate_part, up_part, down_part = piece
            terms = (jnp.dot(token_part, gate_part, preferred_element_type=jnp.float32),
                     jnp.dot(token_part, up_part, preferred_element_type=jnp.float32),
                     lax.dot_general(cotan_part, down_part, (((1,), (1,)), ((), ())), preferred_element_type=jnp.float32))
            updated = tuple(total + lax.optimization_barrier(term.astype(jnp.bfloat16)).astype(jnp.float32) for total, term in zip(running, terms))
            return updated, None

        start = tuple(jnp.zeros((slots, F), jnp.float32) for count in range(3))
        summed, unused = lax.scan(add_block, start, (token_blocks, cotan_blocks, gate_blocks, up_blocks, down_blocks))
        gate_pre, up_pre, act_grad = summed
        sigmoid = jax.nn.sigmoid(gate_pre)
        gate_grad = (act_grad * up_pre * sigmoid * (1.0 + gate_pre * (1.0 - sigmoid))).astype(jnp.bfloat16)
        up_grad = (act_grad * gate_pre * sigmoid).astype(jnp.bfloat16)
        gate_total = lax.dot_general(token_rows, gate_grad, (((0,), (0,)), ((), ())), preferred_element_type=jnp.float32)
        up_total = lax.dot_general(token_rows, up_grad, (((0,), (0,)), ((), ())), preferred_element_type=jnp.float32)
        return gate_total.astype(jnp.bfloat16), up_total.astype(jnp.bfloat16)

    gate_all, up_all = lax.map(one_expert, jnp.arange(EXPERTS, dtype=jnp.int32))
    grad_gate = gate_all.transpose(1, 0, 2).reshape(D, EXPERTS * F)
    grad_up = up_all.transpose(1, 0, 2).reshape(D, EXPERTS * F)
    return (grad_gate, grad_up)
```

```python
import jax
import jax.numpy as jnp
from jax import lax
from jax.experimental import pallas as pl
from jax.experimental.pallas import tpu as pltpu
from jax.sharding import Mesh, PartitionSpec as P

SLICES = 4
CORES = 2
LANES = 128
MAIN = 8
VMEM = pltpu.VMEM
F32 = jnp.float32
BF16 = jnp.bfloat16


def whole(count):
    return [pl.BlockSpec(memory_space=VMEM)] * count


def pack_kernel(capacity, routes_ref, weight_ref, tokens_ref, grad_ref, out_ref, rows_ref):
    width, count = tokens_ref.shape
    experts = out_ref.shape[0] // SLICES
    chunks = 2 * width // LANES
    extra = capacity - MAIN
    tail_rows = out_ref.shape[1] - chunks * MAIN
    rows_ref[:width] = (weight_ref[...].astype(F32) * grad_ref[...].astype(F32)).astype(BF16)
    rows_ref[width:] = tokens_ref[...]
    expert = routes_ref[...]
    onehot = (expert == lax.broadcasted_iota(jnp.int32, (experts, count), 0)).astype(F32)
    earlier = lax.broadcasted_iota(jnp.int32, (count, count), 0)
    later = lax.broadcasted_iota(jnp.int32, (count, count), 1)
    before = jnp.dot(onehot, (earlier < later).astype(F32), preferred_element_type=F32)
    slot = jnp.sum(onehot * before, axis=0, keepdims=True).astype(jnp.int32)
    contract = (((1,), (1,)), ((), ()))
    place = lax.broadcasted_iota(jnp.int32, (experts * MAIN, count), 0)
    main_pick = ((slot < MAIN) & (expert * MAIN + slot == place)).astype(F32).astype(BF16)
    main = lax.dot_general(main_pick, rows_ref[...], contract, preferred_element_type=F32)
    place = lax.broadcasted_iota(jnp.int32, (experts * tail_rows, count), 0)
    tail = jnp.zeros((experts * tail_rows, LANES), F32)
    for c in range(chunks):
        target = expert * tail_rows + c * extra + slot - MAIN
        pick = ((slot >= MAIN) & (target == place)).astype(F32).astype(BF16)
        tail = tail + lax.dot_general(
            pick, rows_ref[c * LANES : (c + 1) * LANES], contract, preferred_element_type=F32
        )
    for e in range(experts):
        pieces = [
            main[e * MAIN : (e + 1) * MAIN, c * LANES : (c + 1) * LANES] for c in range(chunks)
        ]
        pieces.append(tail[e * tail_rows : (e + 1) * tail_rows])
        block = jnp.concatenate(pieces, axis=0).astype(BF16)
        for copy in range(SLICES):
            out_ref[e * SLICES + copy] = block


def partial_kernel(
    capacity, step, core_ref, arrived_ref, gate_ref, up_ref, down_ref,
    rows_ref, send_ref, keep_ref, gate_up_ref, down_pad_ref,
):
    sources, block_rows, _ = arrived_ref.shape
    slots, width = rows_ref.shape
    half = slots // CORES
    chunks = width // LANES
    depth, hidden = gate_ref.shape
    wide = gate_up_ref.shape[0]
    extra = capacity - MAIN
    tail_rows = block_rows - chunks * MAIN
    gate_up_ref[: wide - depth] = jnp.zeros((wide - depth, 2 * hidden), BF16)
    gate_up_ref[wide - depth :, :hidden] = gate_ref[...]
    gate_up_ref[wide - depth :, hidden:] = up_ref[...]
    down_pad_ref[depth:] = jnp.zeros((wide - depth, hidden), BF16)
    down_pad_ref[:depth] = down_ref[...]

    def unpack(pair, carry):
        first = arrived_ref[2 * pair][: chunks * MAIN].astype(F32)
        second = arrived_ref[2 * pair + 1][: chunks * MAIN].astype(F32)
        at = pl.multiple_of(pair * 2 * MAIN, 2 * MAIN)
        for c in range(chunks):
            both = jnp.concatenate(
                [first[c * MAIN : (c + 1) * MAIN], second[c * MAIN : (c + 1) * MAIN]], axis=0
            )
            rows_ref[pl.ds(at, 2 * MAIN), c * LANES : (c + 1) * LANES] = both.astype(BF16)
        return carry

    lax.fori_loop(0, sources // 2, unpack, 0, unroll=4)
    group = 16
    place = lax.broadcasted_iota(jnp.int32, (chunks * group * extra, group * tail_rows), 0)
    origin = lax.broadcasted_iota(jnp.int32, (chunks * group * extra, group * tail_rows), 1)
    chunk = place // (group * extra)
    inside = place % (group * extra)
    wanted = (inside // extra) * tail_rows + chunk * extra + inside % extra
    pick = (wanted == origin).astype(F32).astype(BF16)
    for g in range(sources // group):
        tails = [
            arrived_ref[g * group + s].astype(F32)[chunks * MAIN :] for s in range(group)
        ]
        tail = jnp.concatenate(tails, axis=0).astype(BF16)
        moved = jnp.dot(pick, tail, preferred_element_type=F32).astype(BF16)
        at = sources * MAIN + g * group * extra
        for c in range(chunks):
            rows_ref[at : at + group * extra, c * LANES : (c + 1) * LANES] = moved[
                c * group * extra : (c + 1) * group * extra
            ]

    core = core_ref[0]

    def multiply(start, out_ref):
        for i in range(half // step):
            at = pl.multiple_of(start + i * step, 16)
            token_part = rows_ref[pl.ds(at, step), width - wide :]
            cotan_part = rows_ref[pl.ds(at, step), :wide]
            here = slice(i * step, (i + 1) * step)
            out_ref[here, : 2 * hidden] = jnp.dot(
                token_part, gate_up_ref[...], preferred_element_type=F32
            ).astype(BF16)
            out_ref[here, 2 * hidden :] = jnp.dot(
                cotan_part, down_pad_ref[...], preferred_element_type=F32
            ).astype(BF16)

    multiply((1 - core) * half, send_ref)
    multiply(core * half, keep_ref)


def factor_kernel(parts_ref, out_ref):
    parts, _, columns = parts_ref.shape
    hidden = columns // 3
    total = parts_ref[0].astype(F32)
    for j in range(1, parts):
        total = total + parts_ref[j].astype(F32)
    gate_pre = total[:, :hidden]
    up_pre = total[:, hidden : 2 * hidden]
    act_grad = total[:, 2 * hidden :]
    sigmoid = 1.0 / (1.0 + jnp.exp(-gate_pre))
    gate_grad = (act_grad * up_pre * sigmoid * (1.0 + gate_pre * (1.0 - sigmoid))).astype(BF16)
    up_grad = (act_grad * gate_pre * sigmoid).astype(BF16)
    for j in range(out_ref.shape[0]):
        out_ref[j, :, :hidden] = gate_grad
        out_ref[j, :, hidden:] = up_grad


def weight_kernel(core_ref, rows_ref, own_ref, other_ref, gate_ref, up_ref):
    slots, width = rows_ref.shape
    depth, hidden = gate_ref.shape
    half = slots // CORES
    wide = -(-depth // LANES) * LANES
    core = core_ref[0]
    own_at = pl.multiple_of(core * half, 16)
    other_at = pl.multiple_of((1 - core) * half, 16)
    own_rows = rows_ref[pl.ds(own_at, half), width - wide :]
    other_rows = rows_ref[pl.ds(other_at, half), width - wide :]
    contract = (((0,), (0,)), ((), ()))
    for out_ref, left in ((gate_ref, 0), (up_ref, hidden)):
        block = slice(left, left + hidden)
        total = lax.dot_general(own_rows, own_ref[:, block], contract, preferred_element_type=F32)
        total = total + lax.dot_general(
            other_rows, other_ref[:, block], contract, preferred_element_type=F32
        )
        out_ref[...] = total[wide - depth :].astype(BF16)


def shards(tokens, routes, route_weight, out_grad, w_gate, w_up, w_down):
    columns = lax.axis_size("expert")
    chips = lax.axis_size("chip")
    experts = columns // SLICES
    count, depth = tokens.shape
    hidden = w_gate.shape[1]
    width = 2 * depth
    chunks = width // LANES
    capacity = max(2, count * 5 // (experts * 4))
    slots = columns * capacity
    half = slots // CORES
    block_rows = chunks * MAIN + -(-chunks * (capacity - MAIN) // 8) * 8
    wide = -(-depth // LANES) * LANES
    core = lax.axis_index("core").astype(jnp.int32).reshape(1)
    pairs = [(c, (c + 1) % CORES) for c in range(CORES)]
    smem = pl.BlockSpec(memory_space=pltpu.SMEM)

    blocks = pl.pallas_call(
        lambda *refs: pack_kernel(capacity, *refs),
        out_shape=jax.ShapeDtypeStruct((columns, block_rows, LANES), BF16),
        in_specs=whole(4),
        out_specs=whole(1)[0],
        scratch_shapes=[VMEM((width, count), BF16)],
        compiler_params=pltpu.CompilerParams(vmem_limit_bytes=16 << 20),
        name="pack",
    )(routes.T, route_weight.T, tokens.T, out_grad.T)
    arrived = lax.all_to_all(blocks, "expert", split_axis=0, concat_axis=0, tiled=True)
    rows, send, keep = pl.pallas_call(
        lambda *refs: partial_kernel(capacity, 80, *refs),
        out_shape=(
            jax.ShapeDtypeStruct((slots, width), BF16),
            jax.ShapeDtypeStruct((half, 3 * hidden), BF16),
            jax.ShapeDtypeStruct((half, 3 * hidden), BF16),
        ),
        in_specs=[smem] + whole(4),
        out_specs=tuple(whole(3)),
        scratch_shapes=[VMEM((wide, 2 * hidden), BF16), VMEM((wide, hidden), BF16)],
        compiler_params=pltpu.CompilerParams(vmem_limit_bytes=24 << 20),
        name="partial",
    )(core, arrived, w_gate, w_up, w_down.T)
    sibling = lax.ppermute(send, "core", pairs)
    summed = (keep.astype(F32) + sibling.astype(F32)).astype(BF16)
    parts = lax.all_to_all(
        summed.reshape(chips, half // chips, 3 * hidden),
        "chip", split_axis=0, concat_axis=0, tiled=True,
    )
    spread = pl.pallas_call(
        factor_kernel,
        out_shape=jax.ShapeDtypeStruct((chips, half // chips, 2 * hidden), BF16),
        in_specs=whole(1),
        out_specs=whole(1)[0],
        compiler_params=pltpu.CompilerParams(vmem_limit_bytes=16 << 20),
        name="factor",
    )(parts)
    own = lax.all_to_all(
        spread, "chip", split_axis=0, concat_axis=0, tiled=True
    ).reshape(half, 2 * hidden)
    other = lax.ppermute(own, "core", pairs)
    return pl.pallas_call(
        weight_kernel,
        out_shape=(
            jax.ShapeDtypeStruct((depth, hidden), BF16),
            jax.ShapeDtypeStruct((depth, hidden), BF16),
        ),
        in_specs=[smem] + whole(3),
        out_specs=tuple(whole(2)),
        compiler_params=pltpu.CompilerParams(vmem_limit_bytes=24 << 20),
        name="weight",
    )(core, rows, own, other)


def solution(mesh):
    devices = mesh.devices
    columns, members = devices.shape
    split = Mesh(devices.reshape(columns, members // CORES, CORES), ("expert", "chip", "core"))
    width = ("chip", "core")
    in_specs = (
        P("expert", width),
        P("expert", None),
        P("expert", None),
        P("expert", width),
        P(width, "expert"),
        P(width, "expert"),
        P("expert", width),
    )
    out_specs = (P(width, "expert"), P(width, "expert"))
    return jax.shard_map(shards, mesh=split, in_specs=in_specs, out_specs=out_specs, check_vma=False)
```

```python
import jax
import jax.numpy as jnp
from jax import lax
from jax.experimental import pallas as pl
from jax.experimental.pallas import tpu as pltpu
from jax.sharding import Mesh, PartitionSpec as P

SLICES = 4
CORES = 2
LANES = 128
MAIN = 8
VMEM = pltpu.VMEM
F32 = jnp.float32
BF16 = jnp.bfloat16


def whole(count):
    return [pl.BlockSpec(memory_space=VMEM)] * count


def apart(count):
    return [pl.BlockSpec(memory_space=pltpu.HBM)] * count


def pack_kernel(
    capacity, core_ref, routes_hbm, weight_hbm, tokens_hbm, grad_hbm, out_ref,
    routes_ref, weight_ref, rows_ref, grad_ref, sems,
):
    width, count = grad_ref.shape
    pairs = (
        (routes_hbm, routes_ref),
        (weight_hbm, weight_ref),
        (grad_hbm, grad_ref),
        (tokens_hbm, rows_ref.at[pl.ds(width, width)]),
    )
    copies = [pltpu.make_async_copy(a, b, sems.at[i]) for i, (a, b) in enumerate(pairs)]
    for copy in copies:
        copy.start()
    experts = out_ref.shape[0] // SLICES
    chunks = 2 * width // LANES
    extra = capacity - MAIN
    tail_rows = out_ref.shape[1] - chunks * MAIN
    earlier = lax.broadcasted_iota(jnp.int32, (count, count), 0)
    later = lax.broadcasted_iota(jnp.int32, (count, count), 1)
    order = (earlier < later).astype(F32)
    copies[0].wait()
    expert = routes_ref[...]
    onehot = (expert == lax.broadcasted_iota(jnp.int32, (experts, count), 0)).astype(F32)
    before = jnp.dot(onehot, order, preferred_element_type=F32)
    slot = jnp.sum(onehot * before, axis=0, keepdims=True).astype(jnp.int32)
    contract = (((1,), (1,)), ((), ()))
    place = lax.broadcasted_iota(jnp.int32, (experts * MAIN, count), 0)
    main_pick = ((slot < MAIN) & (expert * MAIN + slot == place)).astype(F32).astype(BF16)
    for copy in copies[1:]:
        copy.wait()
    rows_ref[:width] = (weight_ref[...].astype(F32) * grad_ref[...].astype(F32)).astype(BF16)
    main = lax.dot_general(main_pick, rows_ref[...], contract, preferred_element_type=F32)
    place = lax.broadcasted_iota(jnp.int32, (experts * tail_rows, count), 0)
    tail = jnp.zeros((experts * tail_rows, LANES), F32)
    for c in range(chunks):
        target = expert * tail_rows + c * extra + slot - MAIN
        pick = ((slot >= MAIN) & (target == place)).astype(F32).astype(BF16)
        tail = tail + lax.dot_general(
            pick, rows_ref[c * LANES : (c + 1) * LANES], contract, preferred_element_type=F32
        )
    for e in range(experts):
        pieces = [
            main[e * MAIN : (e + 1) * MAIN, c * LANES : (c + 1) * LANES] for c in range(chunks)
        ]
        pieces.append(tail[e * tail_rows : (e + 1) * tail_rows])
        block = jnp.concatenate(pieces, axis=0).astype(BF16)
        for copy in range(SLICES):
            seat = e * SLICES + copy
            turned = (seat + out_ref.shape[0] // 2) % out_ref.shape[0]
            out_ref[jnp.where(core_ref[0] == 0, seat, turned)] = block


def multiply(rows_ref, gate_up_ref, down_ref, start, step, out_ref):
    wide, pair = gate_up_ref.shape
    width = rows_ref.shape[1]
    for i in range(out_ref.shape[0] // step):
        at = pl.multiple_of(start + i * step, 16)
        here = slice(i * step, (i + 1) * step)
        out_ref[here, :pair] = jnp.dot(
            rows_ref[pl.ds(at, step), width - wide :], gate_up_ref[...], preferred_element_type=F32
        ).astype(BF16)
        out_ref[here, pair:] = jnp.dot(
            rows_ref[pl.ds(at, step), :wide], down_ref[...], preferred_element_type=F32
        ).astype(BF16)


def send_kernel(
    capacity, step, core_ref, arrived_ref, gate_hbm, up_hbm, down_hbm,
    rows_ref, send_ref, gate_up_ref, down_ref, sems,
):
    sources, block_rows, _ = arrived_ref.shape
    slots, width = rows_ref.shape
    half = slots // CORES
    chunks = width // LANES
    depth, hidden = gate_hbm.shape
    wide = gate_up_ref.shape[0]
    extra = capacity - MAIN
    tail_rows = block_rows - chunks * MAIN
    pairs = (
        (gate_hbm, gate_up_ref.at[pl.ds(wide - depth, depth), pl.ds(0, hidden)]),
        (up_hbm, gate_up_ref.at[pl.ds(wide - depth, depth), pl.ds(hidden, hidden)]),
        (down_hbm, down_ref.at[pl.ds(0, depth)]),
    )
    copies = [pltpu.make_async_copy(a, b, sems.at[i]) for i, (a, b) in enumerate(pairs)]
    for copy in copies:
        copy.start()
    gate_up_ref[: wide - depth] = jnp.zeros((wide - depth, 2 * hidden), BF16)
    down_ref[depth:] = jnp.zeros((wide - depth, hidden), BF16)

    turn = core_ref[0] * (sources // 2)
    block_of = lambda source: arrived_ref[lax.rem(turn + source, sources)].astype(F32)

    def unpack(pair, carry):
        first = block_of(2 * pair)[: chunks * MAIN]
        second = block_of(2 * pair + 1)[: chunks * MAIN]
        at = pl.multiple_of(pair * 2 * MAIN, 2 * MAIN)
        for c in range(chunks):
            both = jnp.concatenate(
                [first[c * MAIN : (c + 1) * MAIN], second[c * MAIN : (c + 1) * MAIN]], axis=0
            )
            rows_ref[pl.ds(at, 2 * MAIN), c * LANES : (c + 1) * LANES] = both.astype(BF16)
        return carry

    lax.fori_loop(0, sources // 2, unpack, 0, unroll=4)
    group = 16
    place = lax.broadcasted_iota(jnp.int32, (chunks * group * extra, group * tail_rows), 0)
    origin = lax.broadcasted_iota(jnp.int32, (chunks * group * extra, group * tail_rows), 1)
    chunk = place // (group * extra)
    inside = place % (group * extra)
    wanted = (inside // extra) * tail_rows + chunk * extra + inside % extra
    pick = (wanted == origin).astype(F32).astype(BF16)
    for g in range(sources // group):
        tails = [block_of(g * group + s)[chunks * MAIN :] for s in range(group)]
        tail = jnp.concatenate(tails, axis=0).astype(BF16)
        moved = jnp.dot(pick, tail, preferred_element_type=F32).astype(BF16)
        at = sources * MAIN + g * group * extra
        for c in range(chunks):
            rows_ref[at : at + group * extra, c * LANES : (c + 1) * LANES] = moved[
                c * group * extra : (c + 1) * group * extra
            ]
    for copy in copies:
        copy.wait()
    multiply(rows_ref, gate_up_ref, down_ref, (1 - core_ref[0]) * half, step, send_ref)


def keep_kernel(step, core_ref, rows_ref, gate_up_ref, down_ref, keep_ref):
    multiply(rows_ref, gate_up_ref, down_ref, core_ref[0] * keep_ref.shape[0], step, keep_ref)


def factor_kernel(parts_ref, out_ref):
    parts, _, columns = parts_ref.shape
    hidden = columns // 3
    total = parts_ref[0].astype(F32)
    for j in range(1, parts):
        total = total + parts_ref[j].astype(F32)
    gate_pre = total[:, :hidden]
    up_pre = total[:, hidden : 2 * hidden]
    act_grad = total[:, 2 * hidden :]
    sigmoid = 1.0 / (1.0 + jnp.exp(-gate_pre))
    gate_grad = (act_grad * up_pre * sigmoid * (1.0 + gate_pre * (1.0 - sigmoid))).astype(BF16)
    up_grad = (act_grad * gate_pre * sigmoid).astype(BF16)
    for j in range(out_ref.shape[0]):
        out_ref[j, :, :hidden] = gate_grad
        out_ref[j, :, hidden:] = up_grad


def outer(rows_ref, factor_ref, start, wide):
    half = factor_ref.shape[0]
    rows = rows_ref[pl.ds(pl.multiple_of(start, 16), half), rows_ref.shape[1] - wide :]
    return lax.dot_general(
        rows, factor_ref[...], (((0,), (0,)), ((), ())), preferred_element_type=F32
    )


def own_kernel(core_ref, rows_ref, own_ref, total_ref):
    start = core_ref[0] * own_ref.shape[0]
    total_ref[...] = outer(rows_ref, own_ref, start, total_ref.shape[0])


def other_kernel(core_ref, rows_ref, other_ref, total_ref, gate_ref, up_ref):
    wide = total_ref.shape[0]
    depth, hidden = gate_ref.shape
    start = (1 - core_ref[0]) * other_ref.shape[0]
    total = total_ref[...] + outer(rows_ref, other_ref, start, wide)
    gate_ref[...] = total[wide - depth :, :hidden].astype(BF16)
    up_ref[...] = total[wide - depth :, hidden:].astype(BF16)


def shards(tokens, routes, route_weight, out_grad, w_gate, w_up, w_down):
    columns = lax.axis_size("expert")
    chips = lax.axis_size("chip")
    experts = columns // SLICES
    count, depth = tokens.shape
    hidden = w_gate.shape[1]
    width = 2 * depth
    chunks = width // LANES
    capacity = max(2, count * 5 // (experts * 4))
    slots = columns * capacity
    half = slots // CORES
    block_rows = chunks * MAIN + -(-chunks * (capacity - MAIN) // 8) * 8
    wide = -(-depth // LANES) * LANES
    core = lax.axis_index("core").astype(jnp.int32).reshape(1)
    turned = [*range(columns // 2, columns), *range(columns // 2)]
    planes = [[e * CORES for e in range(columns)], [e * CORES + 1 for e in turned]]
    walk = [*range(0, chips, 2), *range(1, chips, 2)]
    rings = [[chip * CORES for chip in walk], [chip * CORES + 1 for chip in reversed(walk)]]
    pairs = [(c, (c + 1) % CORES) for c in range(CORES)]
    smem = pl.BlockSpec(memory_space=pltpu.SMEM)

    limit = pltpu.CompilerParams(vmem_limit_bytes=24 << 20)
    most = pltpu.CompilerParams(vmem_limit_bytes=56 << 20)

    blocks = pl.pallas_call(
        lambda *refs: pack_kernel(capacity, *refs),
        out_shape=jax.ShapeDtypeStruct((columns, block_rows, LANES), BF16),
        in_specs=[smem] + apart(4),
        out_specs=whole(1)[0],
        scratch_shapes=[
            VMEM((1, count), jnp.int32),
            VMEM((1, count), BF16),
            VMEM((width, count), BF16),
            VMEM((depth, count), BF16),
            pltpu.SemaphoreType.DMA((4,)),
        ],
        compiler_params=most,
        name="pack",
    )(core, routes.T, route_weight.T, tokens.T, out_grad.T)
    arrived = lax.all_to_all(
        blocks, ("expert", "core"), split_axis=0, concat_axis=0, axis_index_groups=planes, tiled=True
    )
    rows, send, gate_up, down = pl.pallas_call(
        lambda *refs: send_kernel(capacity, 80, *refs),
        out_shape=(
            jax.ShapeDtypeStruct((slots, width), BF16),
            jax.ShapeDtypeStruct((half, 3 * hidden), BF16),
            jax.ShapeDtypeStruct((wide, 2 * hidden), BF16),
            jax.ShapeDtypeStruct((wide, hidden), BF16),
        ),
        in_specs=[smem] + whole(1) + apart(3),
        out_specs=tuple(whole(4)),
        scratch_shapes=[pltpu.SemaphoreType.DMA((3,))],
        compiler_params=limit,
        name="send",
    )(core, arrived, w_gate, w_up, w_down.T)
    sibling = lax.ppermute(send, "core", pairs)
    keep = pl.pallas_call(
        lambda *refs: keep_kernel(80, *refs),
        out_shape=jax.ShapeDtypeStruct((half, 3 * hidden), BF16),
        in_specs=[smem] + whole(3),
        out_specs=whole(1)[0],
        compiler_params=limit,
        cost_estimate=pl.CostEstimate(
            flops=6 * half * wide * hidden, bytes_accessed=8 << 20, transcendentals=0
        ),
        name="keep",
    )(core, rows, gate_up, down)
    summed = (keep.astype(F32) + sibling.astype(F32)).astype(BF16)
    parts = lax.all_to_all(
        summed.reshape(chips, half // chips, 3 * hidden),
        ("chip", "core"), split_axis=0, concat_axis=0, axis_index_groups=rings, tiled=True,
    )
    spread = pl.pallas_call(
        factor_kernel,
        out_shape=jax.ShapeDtypeStruct((chips, half // chips, 2 * hidden), BF16),
        in_specs=whole(1),
        out_specs=whole(1)[0],
        compiler_params=limit,
        name="factor",
    )(parts)
    own = lax.all_to_all(
        spread, ("chip", "core"), split_axis=0, concat_axis=0, axis_index_groups=rings, tiled=True
    ).reshape(half, 2 * hidden)
    other = lax.ppermute(own, "core", pairs)
    total = pl.pallas_call(
        own_kernel,
        out_shape=jax.ShapeDtypeStruct((wide, 2 * hidden), F32),
        in_specs=[smem] + whole(2),
        out_specs=whole(1)[0],
        compiler_params=limit,
        cost_estimate=pl.CostEstimate(
            flops=4 * half * wide * hidden, bytes_accessed=8 << 20, transcendentals=0
        ),
        name="own",
    )(core, rows, own)
    return pl.pallas_call(
        other_kernel,
        out_shape=(
            jax.ShapeDtypeStruct((depth, hidden), BF16),
            jax.ShapeDtypeStruct((depth, hidden), BF16),
        ),
        in_specs=[smem] + whole(3),
        out_specs=tuple(whole(2)),
        compiler_params=limit,
        name="other",
    )(core, rows, other, total)


def solution(mesh):
    devices = mesh.devices
    columns, members = devices.shape
    split = Mesh(devices.reshape(columns, members // CORES, CORES), ("expert", "chip", "core"))
    width = ("chip", "core")
    in_specs = (
        P("expert", width),
        P("expert", None),
        P("expert", None),
        P("expert", width),
        P(width, "expert"),
        P(width, "expert"),
        P("expert", width),
    )
    out_specs = (P(width, "expert"), P(width, "expert"))
    return jax.shard_map(shards, mesh=split, in_specs=in_specs, out_specs=out_specs, check_vma=False)
```

```python
import jax
import jax.numpy as jnp
from jax import lax
from jax.experimental import pallas as pl
from jax.experimental.pallas import tpu as pltpu
from jax.sharding import Mesh, PartitionSpec as P

SLICES = 4
CORES = 2
LANES = 128
MAIN = 8
VMEM = pltpu.VMEM
F32 = jnp.float32
BF16 = jnp.bfloat16


def whole(count):
    return [pl.BlockSpec(memory_space=VMEM)] * count


def apart(count):
    return [pl.BlockSpec(memory_space=pltpu.HBM)] * count


def pack_kernel(
    capacity, core_ref, routes_hbm, weight_hbm, tokens_hbm, grad_hbm, out_ref,
    routes_ref, weight_ref, rows_ref, grad_ref, sems,
):
    width, count = grad_ref.shape
    pairs = (
        (routes_hbm, routes_ref),
        (weight_hbm, weight_ref),
        (grad_hbm, grad_ref),
        (tokens_hbm, rows_ref.at[pl.ds(width, width)]),
    )
    copies = [pltpu.make_async_copy(a, b, sems.at[i]) for i, (a, b) in enumerate(pairs)]
    for copy in copies:
        copy.start()
    experts = out_ref.shape[0] // SLICES
    chunks = 2 * width // LANES
    extra = capacity - MAIN
    tail_rows = out_ref.shape[1] - chunks * MAIN
    earlier = lax.broadcasted_iota(jnp.int32, (count, count), 0)
    later = lax.broadcasted_iota(jnp.int32, (count, count), 1)
    order = (earlier < later).astype(F32)
    copies[0].wait()
    expert = routes_ref[...]
    onehot = (expert == lax.broadcasted_iota(jnp.int32, (experts, count), 0)).astype(F32)
    before = jnp.dot(onehot, order, preferred_element_type=F32)
    slot = jnp.sum(onehot * before, axis=0, keepdims=True).astype(jnp.int32)
    contract = (((1,), (1,)), ((), ()))
    place = lax.broadcasted_iota(jnp.int32, (experts * MAIN, count), 0)
    main_pick = ((slot < MAIN) & (expert * MAIN + slot == place)).astype(F32).astype(BF16)
    for copy in copies[1:]:
        copy.wait()
    rows_ref[:width] = (weight_ref[...].astype(F32) * grad_ref[...].astype(F32)).astype(BF16)
    main = lax.dot_general(main_pick, rows_ref[...], contract, preferred_element_type=F32)
    place = lax.broadcasted_iota(jnp.int32, (experts * tail_rows, count), 0)
    tail = jnp.zeros((experts * tail_rows, LANES), F32)
    for c in range(chunks):
        target = expert * tail_rows + c * extra + slot - MAIN
        pick = ((slot >= MAIN) & (target == place)).astype(F32).astype(BF16)
        tail = tail + lax.dot_general(
            pick, rows_ref[c * LANES : (c + 1) * LANES], contract, preferred_element_type=F32
        )
    for e in range(experts):
        pieces = [
            main[e * MAIN : (e + 1) * MAIN, c * LANES : (c + 1) * LANES] for c in range(chunks)
        ]
        pieces.append(tail[e * tail_rows : (e + 1) * tail_rows])
        block = jnp.concatenate(pieces, axis=0).astype(BF16)
        for copy in range(SLICES):
            seat = e * SLICES + copy
            last = out_ref.shape[0] - 1 - seat
            out_ref[jnp.where(core_ref[0] == 0, seat, last)] = block


def unpack(capacity, core_ref, half, arrived_ref, rows_ref):
    sources, block_rows, _ = arrived_ref.shape
    width = rows_ref.shape[1]
    members = sources // CORES
    chunks = width // LANES
    extra = capacity - MAIN
    tail_rows = block_rows - chunks * MAIN
    first_core = core_ref[0] == 0

    def block_of(source):
        source = half * members + source
        return arrived_ref[jnp.where(first_core, source, sources - 1 - source)].astype(F32)

    def main_rows(pair, carry):
        first = block_of(2 * pair)
        second = block_of(2 * pair + 1)
        at = pl.multiple_of(pair * 2 * MAIN, 2 * MAIN)
        for c in range(chunks):
            here = slice(c * MAIN, (c + 1) * MAIN)
            both = jnp.concatenate([first[here], second[here]], axis=0)
            rows_ref[pl.ds(at, 2 * MAIN), c * LANES : (c + 1) * LANES] = both.astype(BF16)
        return carry

    lax.fori_loop(0, members // 2, main_rows, 0, unroll=4)
    group = 16
    size = group * extra
    place = lax.broadcasted_iota(jnp.int32, (chunks * size, group * tail_rows), 0)
    origin = lax.broadcasted_iota(jnp.int32, (chunks * size, group * tail_rows), 1)
    inside = place % size
    wanted = (inside // extra) * tail_rows + place // size * extra + inside % extra
    pick = (wanted == origin).astype(F32).astype(BF16)
    for g in range(members // group):
        tails = [block_of(g * group + s)[chunks * MAIN :] for s in range(group)]
        tail = jnp.concatenate(tails, axis=0).astype(BF16)
        moved = jnp.dot(pick, tail, preferred_element_type=F32).astype(BF16)
        at = members * MAIN + g * size
        for c in range(chunks):
            rows_ref[at : at + size, c * LANES : (c + 1) * LANES] = moved[c * size : (c + 1) * size]


def multiply(rows_ref, gate_up_ref, down_ref, step, out_ref):
    wide, pair = gate_up_ref.shape
    width = rows_ref.shape[1]
    for at in range(0, out_ref.shape[0], step):
        here = slice(at, at + step)
        out_ref[here, :pair] = jnp.dot(
            rows_ref[here, width - wide :], gate_up_ref[...], preferred_element_type=F32
        ).astype(BF16)
        out_ref[here, pair:] = jnp.dot(
            rows_ref[here, :wide], down_ref[...], preferred_element_type=F32
        ).astype(BF16)


def send_kernel(
    capacity, step, core_ref, arrived_ref, gate_hbm, up_hbm, down_hbm,
    rows_ref, send_ref, gate_up_ref, down_ref, sems,
):
    depth, hidden = gate_hbm.shape
    wide = gate_up_ref.shape[0]
    pairs = (
        (gate_hbm, gate_up_ref.at[pl.ds(wide - depth, depth), pl.ds(0, hidden)]),
        (up_hbm, gate_up_ref.at[pl.ds(wide - depth, depth), pl.ds(hidden, hidden)]),
        (down_hbm, down_ref.at[pl.ds(0, depth)]),
    )
    copies = [pltpu.make_async_copy(a, b, sems.at[i]) for i, (a, b) in enumerate(pairs)]
    for copy in copies:
        copy.start()
    gate_up_ref[: wide - depth] = jnp.zeros((wide - depth, 2 * hidden), BF16)
    down_ref[depth:] = jnp.zeros((wide - depth, hidden), BF16)
    unpack(capacity, core_ref, 1 - core_ref[0], arrived_ref, rows_ref)
    for copy in copies:
        copy.wait()
    multiply(rows_ref, gate_up_ref, down_ref, step, send_ref)


def keep_kernel(capacity, step, core_ref, arrived_ref, gate_up_ref, down_ref, rows_ref, keep_ref):
    unpack(capacity, core_ref, core_ref[0], arrived_ref, rows_ref)
    multiply(rows_ref, gate_up_ref, down_ref, step, keep_ref)


def factor_kernel(parts_ref, out_ref):
    parts, _, columns = parts_ref.shape
    hidden = columns // 3
    total = parts_ref[0].astype(F32)
    for j in range(1, parts):
        total = total + parts_ref[j].astype(F32)
    gate_pre = total[:, :hidden]
    up_pre = total[:, hidden : 2 * hidden]
    act_grad = total[:, 2 * hidden :]
    sigmoid = 1.0 / (1.0 + jnp.exp(-gate_pre))
    gate_grad = (act_grad * up_pre * sigmoid * (1.0 + gate_pre * (1.0 - sigmoid))).astype(BF16)
    up_grad = (act_grad * gate_pre * sigmoid).astype(BF16)
    for j in range(out_ref.shape[0]):
        out_ref[j, :, :hidden] = gate_grad
        out_ref[j, :, hidden:] = up_grad


def outer(rows_ref, factor_ref, wide):
    rows = rows_ref[:, rows_ref.shape[1] - wide :]
    return lax.dot_general(
        rows, factor_ref[...], (((0,), (0,)), ((), ())), preferred_element_type=F32
    )


def own_kernel(rows_ref, own_ref, total_ref):
    total_ref[...] = outer(rows_ref, own_ref, total_ref.shape[0])


def other_kernel(rows_ref, other_ref, total_ref, gate_ref, up_ref):
    wide = total_ref.shape[0]
    depth, hidden = gate_ref.shape
    total = total_ref[...] + outer(rows_ref, other_ref, wide)
    gate_ref[...] = total[wide - depth :, :hidden].astype(BF16)
    up_ref[...] = total[wide - depth :, hidden:].astype(BF16)


def shards(tokens, routes, route_weight, out_grad, w_gate, w_up, w_down):
    columns = lax.axis_size("expert")
    chips = lax.axis_size("chip")
    experts = columns // SLICES
    count, depth = tokens.shape
    hidden = w_gate.shape[1]
    width = 2 * depth
    chunks = width // LANES
    capacity = max(2, count * 5 // (experts * 4))
    slots = columns * capacity
    half = slots // CORES
    block_rows = chunks * MAIN + -(-chunks * (capacity - MAIN) // 8) * 8
    wide = -(-depth // LANES) * LANES
    core = lax.axis_index("core").astype(jnp.int32).reshape(1)
    line = list(range(columns))
    planes = [[e * CORES for e in line], [e * CORES + 1 for e in reversed(line)]]
    walk = list(range(chips))
    rings = [[chip * CORES for chip in walk], [chip * CORES + 1 for chip in reversed(walk)]]
    pairs = [(c, (c + 1) % CORES) for c in range(CORES)]
    smem = pl.BlockSpec(memory_space=pltpu.SMEM)

    limit = pltpu.CompilerParams(vmem_limit_bytes=24 << 20)
    most = pltpu.CompilerParams(vmem_limit_bytes=56 << 20)

    blocks = pl.pallas_call(
        lambda *refs: pack_kernel(capacity, *refs),
        out_shape=jax.ShapeDtypeStruct((columns, block_rows, LANES), BF16),
        in_specs=[smem] + apart(4),
        out_specs=whole(1)[0],
        scratch_shapes=[
            VMEM((1, count), jnp.int32),
            VMEM((1, count), BF16),
            VMEM((width, count), BF16),
            VMEM((depth, count), BF16),
            pltpu.SemaphoreType.DMA((4,)),
        ],
        compiler_params=most,
        name="pack",
    )(core, routes.T, route_weight.T, tokens.T, out_grad.T)
    arrived = lax.all_to_all(
        blocks, ("expert", "core"), split_axis=0, concat_axis=0, axis_index_groups=planes, tiled=True
    )
    other_rows, send, gate_up, down = pl.pallas_call(
        lambda *refs: send_kernel(capacity, 320, *refs),
        out_shape=(
            jax.ShapeDtypeStruct((half, width), BF16),
            jax.ShapeDtypeStruct((half, 3 * hidden), BF16),
            jax.ShapeDtypeStruct((wide, 2 * hidden), BF16),
            jax.ShapeDtypeStruct((wide, hidden), BF16),
        ),
        in_specs=[smem] + whole(1) + apart(3),
        out_specs=tuple(whole(4)),
        scratch_shapes=[pltpu.SemaphoreType.DMA((3,))],
        compiler_params=limit,
        name="send",
    )(core, arrived, w_gate, w_up, w_down.T)
    sibling = lax.ppermute(send, "core", pairs)
    own_rows, keep = pl.pallas_call(
        lambda *refs: keep_kernel(capacity, 320, *refs),
        out_shape=(
            jax.ShapeDtypeStruct((half, width), BF16),
            jax.ShapeDtypeStruct((half, 3 * hidden), BF16),
        ),
        in_specs=[smem] + whole(3),
        out_specs=tuple(whole(2)),
        compiler_params=limit,
        cost_estimate=pl.CostEstimate(
            flops=6 * half * wide * hidden, bytes_accessed=8 << 20, transcendentals=0
        ),
        name="keep",
    )(core, arrived, gate_up, down)
    summed = (keep.astype(F32) + sibling.astype(F32)).astype(BF16)
    parts = lax.all_to_all(
        summed.reshape(chips, half // chips, 3 * hidden),
        ("chip", "core"), split_axis=0, concat_axis=0, axis_index_groups=rings, tiled=True,
    )
    spread = pl.pallas_call(
        factor_kernel,
        out_shape=jax.ShapeDtypeStruct((chips, half // chips, 2 * hidden), BF16),
        in_specs=whole(1),
        out_specs=whole(1)[0],
        compiler_params=limit,
        name="factor",
    )(parts)
    own = lax.all_to_all(
        spread, ("chip", "core"), split_axis=0, concat_axis=0, axis_index_groups=rings, tiled=True
    ).reshape(half, 2 * hidden)
    other = lax.ppermute(own, "core", pairs)
    total = pl.pallas_call(
        own_kernel,
        out_shape=jax.ShapeDtypeStruct((wide, 2 * hidden), F32),
        in_specs=whole(2),
        out_specs=whole(1)[0],
        compiler_params=limit,
        cost_estimate=pl.CostEstimate(
            flops=4 * half * wide * hidden, bytes_accessed=8 << 20, transcendentals=0
        ),
        name="own",
    )(own_rows, own)
    return pl.pallas_call(
        other_kernel,
        out_shape=(
            jax.ShapeDtypeStruct((depth, hidden), BF16),
            jax.ShapeDtypeStruct((depth, hidden), BF16),
        ),
        in_specs=whole(3),
        out_specs=tuple(whole(2)),
        compiler_params=limit,
        name="other",
    )(other_rows, other, total)


def solution(mesh):
    devices = mesh.devices
    columns, members = devices.shape
    split = Mesh(devices.reshape(columns, members // CORES, CORES), ("expert", "chip", "core"))
    width = ("chip", "core")
    in_specs = (
        P("expert", width),
        P("expert", None),
        P("expert", None),
        P("expert", width),
        P(width, "expert"),
        P(width, "expert"),
        P("expert", width),
    )
    out_specs = (P(width, "expert"), P(width, "expert"))
    return jax.shard_map(shards, mesh=split, in_specs=in_specs, out_specs=out_specs, check_vma=False)
```

```python
import jax
import jax.numpy as jnp
from jax import lax
from jax.experimental import pallas as pl
from jax.experimental.pallas import tpu as pltpu
from jax.sharding import Mesh, PartitionSpec as P

SLICES = 4
CORES = 2
LANES = 128
MAIN = 8
VMEM = pltpu.VMEM
F32 = jnp.float32
BF16 = jnp.bfloat16


def whole(count):
    return [pl.BlockSpec(memory_space=VMEM)] * count


def apart(count):
    return [pl.BlockSpec(memory_space=pltpu.HBM)] * count


def pack_kernel(
    capacity, core_ref, routes_hbm, weight_hbm, tokens_hbm, grad_hbm, out_ref,
    routes_ref, weight_ref, rows_ref, grad_ref, sems,
):
    width, count = grad_ref.shape
    pairs = (
        (routes_hbm, routes_ref),
        (weight_hbm, weight_ref),
        (grad_hbm, grad_ref),
        (tokens_hbm, rows_ref.at[pl.ds(width, width)]),
    )
    copies = [pltpu.make_async_copy(a, b, sems.at[i]) for i, (a, b) in enumerate(pairs)]
    for copy in copies:
        copy.start()
    experts = out_ref.shape[0] // SLICES
    chunks = 2 * width // LANES
    extra = capacity - MAIN
    tail_rows = out_ref.shape[1] - chunks * MAIN
    earlier = lax.broadcasted_iota(jnp.int32, (count, count), 0)
    later = lax.broadcasted_iota(jnp.int32, (count, count), 1)
    order = (earlier < later).astype(F32)
    copies[0].wait()
    expert = routes_ref[...]
    onehot = (expert == lax.broadcasted_iota(jnp.int32, (experts, count), 0)).astype(F32)
    before = jnp.dot(onehot, order, preferred_element_type=F32)
    slot = jnp.sum(onehot * before, axis=0, keepdims=True).astype(jnp.int32)
    contract = (((1,), (1,)), ((), ()))
    place = lax.broadcasted_iota(jnp.int32, (experts * MAIN, count), 0)
    main_pick = ((slot < MAIN) & (expert * MAIN + slot == place)).astype(F32).astype(BF16)
    for copy in copies[1:]:
        copy.wait()
    rows_ref[:width] = (weight_ref[...].astype(F32) * grad_ref[...].astype(F32)).astype(BF16)
    main = lax.dot_general(main_pick, rows_ref[...], contract, preferred_element_type=F32)
    place = lax.broadcasted_iota(jnp.int32, (experts * tail_rows, count), 0)
    tail = jnp.zeros((experts * tail_rows, LANES), F32)
    for c in range(chunks):
        target = expert * tail_rows + c * extra + slot - MAIN
        pick = ((slot >= MAIN) & (target == place)).astype(F32).astype(BF16)
        tail = tail + lax.dot_general(
            pick, rows_ref[c * LANES : (c + 1) * LANES], contract, preferred_element_type=F32
        )
    for e in range(experts):
        pieces = [
            main[e * MAIN : (e + 1) * MAIN, c * LANES : (c + 1) * LANES] for c in range(chunks)
        ]
        pieces.append(tail[e * tail_rows : (e + 1) * tail_rows])
        block = jnp.concatenate(pieces, axis=0).astype(BF16)
        for copy in range(SLICES):
            seat = e * SLICES + copy
            last = out_ref.shape[0] - 1 - seat
            out_ref[jnp.where(core_ref[0] == 0, seat, last)] = block


def unpack(capacity, core_ref, half, arrived_ref, rows_ref):
    sources, block_rows, _ = arrived_ref.shape
    width = rows_ref.shape[1]
    members = sources // CORES
    chunks = width // LANES
    extra = capacity - MAIN
    tail_rows = block_rows - chunks * MAIN
    first_core = core_ref[0] == 0

    def block_of(source):
        source = half * members + source
        return arrived_ref[jnp.where(first_core, source, sources - 1 - source)].astype(F32)

    def main_rows(pair, carry):
        first = block_of(2 * pair)
        second = block_of(2 * pair + 1)
        at = pl.multiple_of(pair * 2 * MAIN, 2 * MAIN)
        for c in range(chunks):
            here = slice(c * MAIN, (c + 1) * MAIN)
            both = jnp.concatenate([first[here], second[here]], axis=0)
            rows_ref[pl.ds(at, 2 * MAIN), c * LANES : (c + 1) * LANES] = both.astype(BF16)
        return carry

    lax.fori_loop(0, members // 2, main_rows, 0, unroll=4)
    group = 16
    size = group * extra
    place = lax.broadcasted_iota(jnp.int32, (chunks * size, group * tail_rows), 0)
    origin = lax.broadcasted_iota(jnp.int32, (chunks * size, group * tail_rows), 1)
    inside = place % size
    wanted = (inside // extra) * tail_rows + place // size * extra + inside % extra
    pick = (wanted == origin).astype(F32).astype(BF16)
    for g in range(members // group):
        tails = [block_of(g * group + s)[chunks * MAIN :] for s in range(group)]
        tail = jnp.concatenate(tails, axis=0).astype(BF16)
        moved = jnp.dot(pick, tail, preferred_element_type=F32).astype(BF16)
        at = members * MAIN + g * size
        for c in range(chunks):
            rows_ref[at : at + size, c * LANES : (c + 1) * LANES] = moved[c * size : (c + 1) * size]


def multiply(rows_ref, gate_up_ref, down_ref, step, out_ref):
    wide, pair = gate_up_ref.shape
    width = rows_ref.shape[1]
    for at in range(0, out_ref.shape[0], step):
        here = slice(at, at + step)
        out_ref[here, :pair] = jnp.dot(
            rows_ref[here, width - wide :], gate_up_ref[...], preferred_element_type=F32
        ).astype(BF16)
        out_ref[here, pair:] = jnp.dot(
            rows_ref[here, :wide], down_ref[...], preferred_element_type=F32
        ).astype(BF16)


def send_kernel(
    capacity, step, core_ref, arrived_ref, gate_hbm, up_hbm, down_hbm,
    rows_ref, send_ref, gate_up_ref, down_ref, sems,
):
    depth, hidden = gate_hbm.shape
    wide = gate_up_ref.shape[0]
    pairs = (
        (gate_hbm, gate_up_ref.at[pl.ds(wide - depth, depth), pl.ds(0, hidden)]),
        (up_hbm, gate_up_ref.at[pl.ds(wide - depth, depth), pl.ds(hidden, hidden)]),
        (down_hbm, down_ref.at[pl.ds(0, depth)]),
    )
    copies = [pltpu.make_async_copy(a, b, sems.at[i]) for i, (a, b) in enumerate(pairs)]
    for copy in copies:
        copy.start()
    gate_up_ref[: wide - depth] = jnp.zeros((wide - depth, 2 * hidden), BF16)
    down_ref[depth:] = jnp.zeros((wide - depth, hidden), BF16)
    unpack(capacity, core_ref, 1 - core_ref[0], arrived_ref, rows_ref)
    for copy in copies:
        copy.wait()
    multiply(rows_ref, gate_up_ref, down_ref, step, send_ref)


def keep_kernel(capacity, step, core_ref, arrived_ref, gate_up_ref, down_ref, rows_ref, keep_ref):
    unpack(capacity, core_ref, core_ref[0], arrived_ref, rows_ref)
    multiply(rows_ref, gate_up_ref, down_ref, step, keep_ref)


def factor_kernel(parts_ref, out_ref):
    parts, _, columns = parts_ref.shape
    hidden = columns // 3
    total = parts_ref[0].astype(F32)
    for j in range(1, parts):
        total = total + parts_ref[j].astype(F32)
    gate_pre = total[:, :hidden]
    up_pre = total[:, hidden : 2 * hidden]
    act_grad = total[:, 2 * hidden :]
    sigmoid = 1.0 / (1.0 + jnp.exp(-gate_pre))
    gate_grad = (act_grad * up_pre * sigmoid * (1.0 + gate_pre * (1.0 - sigmoid))).astype(BF16)
    up_grad = (act_grad * gate_pre * sigmoid).astype(BF16)
    for j in range(out_ref.shape[0]):
        out_ref[j, :, :hidden] = gate_grad
        out_ref[j, :, hidden:] = up_grad


def own_kernel(rows_ref, own_ref, other_rows_ref, total_ref, turned_ref):
    wide = total_ref.shape[0]
    left = rows_ref.shape[1] - wide
    total_ref[...] = lax.dot_general(
        rows_ref[:, left:], own_ref[...], (((0,), (0,)), ((), ())), preferred_element_type=F32
    )
    turned_ref[...] = other_rows_ref[:, left:].T


def other_kernel(turned_ref, other_ref, total_ref, gate_hbm, up_hbm, gate_ref, up_ref, sems):
    wide = total_ref.shape[0]
    depth, hidden = gate_ref.shape
    copies = []
    for i, (block_ref, out_hbm) in enumerate(((gate_ref, gate_hbm), (up_ref, up_hbm))):
        here = slice(i * hidden, (i + 1) * hidden)
        total = total_ref[:, here] + jnp.dot(
            turned_ref[...], other_ref[:, here], preferred_element_type=F32
        )
        block_ref[...] = total[wide - depth :].astype(BF16)
        copies.append(pltpu.make_async_copy(block_ref, out_hbm, sems.at[i]))
        copies[-1].start()
    for copy in copies:
        copy.wait()


def shards(tokens, routes, route_weight, out_grad, w_gate, w_up, w_down):
    columns = lax.axis_size("expert")
    chips = lax.axis_size("chip")
    experts = columns // SLICES
    count, depth = tokens.shape
    hidden = w_gate.shape[1]
    width = 2 * depth
    chunks = width // LANES
    capacity = max(2, count * 5 // (experts * 4))
    slots = columns * capacity
    half = slots // CORES
    block_rows = chunks * MAIN + -(-chunks * (capacity - MAIN) // 8) * 8
    wide = -(-depth // LANES) * LANES
    core = lax.axis_index("core").astype(jnp.int32).reshape(1)
    line = list(range(columns))
    planes = [[e * CORES for e in line], [e * CORES + 1 for e in reversed(line)]]
    walk = list(range(chips))
    rings = [[chip * CORES for chip in walk], [chip * CORES + 1 for chip in reversed(walk)]]
    pairs = [(c, (c + 1) % CORES) for c in range(CORES)]
    smem = pl.BlockSpec(memory_space=pltpu.SMEM)

    limit = pltpu.CompilerParams(vmem_limit_bytes=24 << 20)
    most = pltpu.CompilerParams(vmem_limit_bytes=56 << 20)

    blocks = pl.pallas_call(
        lambda *refs: pack_kernel(capacity, *refs),
        out_shape=jax.ShapeDtypeStruct((columns, block_rows, LANES), BF16),
        in_specs=[smem] + apart(4),
        out_specs=whole(1)[0],
        scratch_shapes=[
            VMEM((1, count), jnp.int32),
            VMEM((1, count), BF16),
            VMEM((width, count), BF16),
            VMEM((depth, count), BF16),
            pltpu.SemaphoreType.DMA((4,)),
        ],
        compiler_params=most,
        name="pack",
    )(core, routes.T, route_weight.T, tokens.T, out_grad.T)
    arrived = lax.all_to_all(
        blocks, ("expert", "core"), split_axis=0, concat_axis=0, axis_index_groups=planes, tiled=True
    )
    other_rows, send, gate_up, down = pl.pallas_call(
        lambda *refs: send_kernel(capacity, 320, *refs),
        out_shape=(
            jax.ShapeDtypeStruct((half, width), BF16),
            jax.ShapeDtypeStruct((half, 3 * hidden), BF16),
            jax.ShapeDtypeStruct((wide, 2 * hidden), BF16),
            jax.ShapeDtypeStruct((wide, hidden), BF16),
        ),
        in_specs=[smem] + whole(1) + apart(3),
        out_specs=tuple(whole(4)),
        scratch_shapes=[pltpu.SemaphoreType.DMA((3,))],
        compiler_params=limit,
        name="send",
    )(core, arrived, w_gate, w_up, w_down.T)
    sibling = lax.ppermute(send, "core", pairs)
    own_rows, keep = pl.pallas_call(
        lambda *refs: keep_kernel(capacity, 320, *refs),
        out_shape=(
            jax.ShapeDtypeStruct((half, width), BF16),
            jax.ShapeDtypeStruct((half, 3 * hidden), BF16),
        ),
        in_specs=[smem] + whole(3),
        out_specs=tuple(whole(2)),
        compiler_params=limit,
        cost_estimate=pl.CostEstimate(
            flops=6 * half * wide * hidden, bytes_accessed=8 << 20, transcendentals=0
        ),
        name="keep",
    )(core, arrived, gate_up, down)
    summed = (keep.astype(F32) + sibling.astype(F32)).astype(BF16)
    parts = lax.all_to_all(
        summed.reshape(chips, half // chips, 3 * hidden),
        ("chip", "core"), split_axis=0, concat_axis=0, axis_index_groups=rings, tiled=True,
    )
    spread = pl.pallas_call(
        factor_kernel,
        out_shape=jax.ShapeDtypeStruct((chips, half // chips, 2 * hidden), BF16),
        in_specs=whole(1),
        out_specs=whole(1)[0],
        compiler_params=limit,
        name="factor",
    )(parts)
    own = lax.all_to_all(
        spread, ("chip", "core"), split_axis=0, concat_axis=0, axis_index_groups=rings, tiled=True
    ).reshape(half, 2 * hidden)
    other = lax.ppermute(own, "core", pairs)
    total, turned = pl.pallas_call(
        own_kernel,
        out_shape=(
            jax.ShapeDtypeStruct((wide, 2 * hidden), F32),
            jax.ShapeDtypeStruct((wide, half), BF16),
        ),
        in_specs=whole(3),
        out_specs=tuple(whole(2)),
        compiler_params=limit,
        cost_estimate=pl.CostEstimate(
            flops=4 * half * wide * hidden, bytes_accessed=8 << 20, transcendentals=0
        ),
        name="own",
    )(own_rows, own, other_rows)
    return pl.pallas_call(
        other_kernel,
        out_shape=(
            jax.ShapeDtypeStruct((depth, hidden), BF16),
            jax.ShapeDtypeStruct((depth, hidden), BF16),
        ),
        in_specs=whole(3),
        out_specs=tuple(apart(2)),
        scratch_shapes=[
            VMEM((depth, hidden), BF16),
            VMEM((depth, hidden), BF16),
            pltpu.SemaphoreType.DMA((2,)),
        ],
        compiler_params=limit,
        name="other",
    )(turned, other, total)


def solution(mesh):
    devices = mesh.devices
    columns, members = devices.shape
    split = Mesh(devices.reshape(columns, members // CORES, CORES), ("expert", "chip", "core"))
    width = ("chip", "core")
    in_specs = (
        P("expert", width),
        P("expert", None),
        P("expert", None),
        P("expert", width),
        P(width, "expert"),
        P(width, "expert"),
        P("expert", width),
    )
    out_specs = (P(width, "expert"), P(width, "expert"))
    return jax.shard_map(shards, mesh=split, in_specs=in_specs, out_specs=out_specs, check_vma=False)
```
